32 devices in a mesh: loop: 4 (over x, core), group: 8 (over z, y).
Axes of the slice: x: 2, y: 2, z: 4, core: 2. Of those that a mesh axis runs over, the one named last changes fastest.
Arguments:
- picture_vectors: bfloat16 [4096, 1152], P(('loop', 'group')), may hold values from -2 to 2
- caption_vectors: bfloat16 [4096, 1152], P(('loop', 'group')), may hold values from -2 to 2
- occupied_slot_tally: int32 [32], replicated, may hold values from 0 to 128, as said below
- sharpness_array: float32 [1], replicated, may hold values from 8 to 12
- offset_shift: float32 [1], replicated, may hold values from -6 to -3
Outputs:
- image_grads: bfloat16 [4096, 1152], P(('loop', 'group'))
- text_grads: bfloat16 [4096, 1152], P(('loop', 'group'))
The draws below stay inside these ranges and needn't reach their ends.
Inputs may be any that keep to these rules, and one draw needn't show every extreme that they name: Each entry is 0, 64 or 128; for every even device index k, occupied_slot_tally[k] + occupied_slot_tally[k + 1] = 128, and some device has 128.
All inputs are finite; a program needn't handle non-finite values.
Results may differ from the reference program's by a relative error of at most 0.0043.
Values may be sent and summed in bfloat16 or wider, within the bound.
A program may use at most 128 MiB of HBM per device.

```python
import math
import jax
import jax.numpy as jnp
from jax import lax

E = 1152
ROWS = 128
HALF = 64
TOKENS = 4096
N_LOOP = 4
N_GROUP = 8


def draw_occupied_slot_tally(key, part):
    key = jax.random.fold_in(key, 11)
    pairs = N_LOOP * N_GROUP // 2
    first_key, second_key, third_key = jax.random.split(key, 3)
    kinds = jax.random.randint(first_key, (pairs,), 0, 3)
    chosen = jax.random.randint(second_key, (), 0, pairs)
    forced = 1 + jax.random.randint(third_key, (), 0, 2)
    kinds = jnp.where(jnp.arange(pairs) == chosen, forced, kinds)
    first = jnp.where(kinds == 0, HALF, jnp.where(kinds == 1, ROWS, 0))
    second = ROWS - first
    return jnp.stack([first, second], axis=1).reshape(-1).astype(jnp.int32)


def shared_parts(key):
    keys = jax.random.split(key, 3)
    clusters = max(TOKENS // 32, 1)
    centers = jax.random.truncated_normal(keys[0], -4.0, 4.0, (clusters, E), jnp.float32)
    labels = jax.random.randint(keys[1], (TOKENS,), 0, clusters)
    paired = jax.random.truncated_normal(keys[2], -4.0, 4.0, (TOKENS, E), jnp.float32)
    return (jnp.take(centers, labels, axis=0), paired)


def row_scales(key, low, high):
    return jnp.exp(jax.random.uniform(key, (TOKENS, 1), jnp.float32, math.log(low), math.log(high)))


def draw_picture_vectors(key, part):
    cluster, paired = shared_parts(key)
    key = jax.random.fold_in(key, 5)
    noise_key, scale_key = jax.random.split(key)
    noise = jax.random.truncated_normal(noise_key, -4.0, 4.0, (TOKENS, E), jnp.float32)
    mixed = 0.5 * cluster + 0.5 * paired + 0.707 * noise
    scales = row_scales(scale_key, 0.5, 2.0)
    return (mixed * scales / math.sqrt(E)).astype(jnp.bfloat16)


def draw_caption_vectors(key, part):
    cluster, paired = shared_parts(key)
    key = jax.random.fold_in(key, 6)
    noise_key, scale_key = jax.random.split(key)
    noise = jax.random.truncated_normal(noise_key, -4.0, 4.0, (TOKENS, E), jnp.float32)
    mixed = 0.5 * cluster + 0.5 * paired + 0.707 * noise
    scales = row_scales(scale_key, 0.5, 2.0)
    return (mixed * scales / math.sqrt(E)).astype(jnp.bfloat16)


def setup_inputs(seed: int = 0) -> dict:
    arg_keys = jax.random.split(jax.random.key(seed), 6)
    return {
        "picture_vectors": draw_picture_vectors(jax.random.fold_in(arg_keys[5], 71), 0),
        "caption_vectors": draw_caption_vectors(jax.random.fold_in(arg_keys[5], 71), 0),
        "occupied_slot_tally": draw_occupied_slot_tally(jax.random.fold_in(arg_keys[5], 71), 0),
        "sharpness_array": jnp.clip(jax.random.uniform(arg_keys[3], (1,), jnp.float32, 8.0, 12.0), 8.0, 12.0),
        "offset_shift": jnp.clip(jax.random.uniform(arg_keys[4], (1,), jnp.float32, -6.0, -3.0), -6.0, -3.0),
    }


def unit_normalize(raw):
    values = raw.astype(jnp.float32)
    inverse = lax.rsqrt(lax.optimization_barrier(jnp.sum(values * values, axis=1, keepdims=True)) + 1e-06)
    return (values * inverse, inverse)

def project(unit, inverse, grads):
    return ((grads - unit * lax.optimization_barrier(jnp.sum(unit * grads, axis=1, keepdims=True))) * inverse).astype(jnp.bfloat16)

def reference(picture_vectors, caption_vectors, occupied_slot_tally, sharpness_array, offset_shift):
    total, width = picture_vectors.shape
    img_unit, img_inv = unit_normalize(picture_vectors)
    txt_unit, text_inverse_norm = unit_normalize(caption_vectors)
    img_half = img_unit.astype(jnp.bfloat16)
    caption_portion = txt_unit.astype(jnp.bfloat16)
    row_ids = jnp.arange(total, dtype=jnp.int32)
    owners = row_ids // ROWS
    live = (row_ids % ROWS < occupied_slot_tally[owners]).astype(jnp.float32)
    sharpness_factor = sharpness_array[0]
    offset = offset_shift[0]

    def step(carry, index):
        start = (index * ROWS).astype(jnp.int32)
        block = lax.dynamic_slice_in_dim(img_half, start, ROWS, 0)
        block_ids = lax.dynamic_slice_in_dim(row_ids, start, ROWS, 0)
        block_live = lax.dynamic_slice_in_dim(live, start, ROWS, 0)
        logits = jnp.dot(block, caption_portion.T, preferred_element_type=jnp.float32) * sharpness_factor + offset
        target = (block_ids[:, None] == row_ids[None, :]).astype(jnp.float32)
        weight = (sharpness_factor * block_live[:, None] * live[None, :] * (jax.nn.sigmoid(logits) - target)).astype(jnp.bfloat16)
        picture_contribution = jnp.dot(weight, caption_portion, preferred_element_type=jnp.float32)
        carry = carry + jnp.dot(weight.T, block, preferred_element_type=jnp.float32)
        return (carry, picture_contribution)
    text_sum, img_terms = lax.scan(step, jnp.zeros((total, width), jnp.float32), jnp.arange(total // ROWS, dtype=jnp.int32))
    img_sum = img_terms.reshape(total, width)
    return (project(img_unit, img_inv, img_sum), project(txt_unit, text_inverse_norm, text_sum))
```

```python
import functools

import jax
import jax.numpy as jnp
from jax import lax
from jax.experimental import pallas as pl
from jax.experimental.pallas import tpu as pltpu
from jax.sharding import PartitionSpec as P

MESH = pl.DeviceIdType.MESH
F32 = jnp.float32
BF16 = jnp.bfloat16


def unit_normalize(raw):
    values = raw.astype(F32)
    inverse = lax.rsqrt(jnp.sum(values * values, axis=1, keepdims=True) + 1e-06)
    return values * inverse, inverse


def project(raw, grads):
    unit, inverse = unit_normalize(raw)
    radial = jnp.sum(unit * grads, axis=1, keepdims=True)
    return ((grads - unit * radial) * inverse).astype(BF16)


def kernel(
    far,
    img_ref,
    txt_ref,
    tally_ref,
    sharp_ref,
    shift_ref,
    img_out,
    txt_out,
    images,
    pair_in,
    pair_own,
    texts,
    weights,
    img_send,
    img_recv,
    img_keep,
    img_send2,
    img_recv2,
    core_send,
    core_recv,
    txt_keep,
    txt_send,
    txt_recv,
    txt_send2,
    txt_recv2,
    last_send,
    last_recv,
    send_sem,
    recv_sem,
):
    rows, width = img_ref.shape
    half = rows // 2
    loop = lax.axis_index("loop")
    group = lax.axis_index("group")
    x, core = loop // 2, loop % 2
    h, z, y = group // 4, (group // 2) % 2, group % 2

    x_peer = (2 * (1 - x) + core, group)
    core_peer = (2 * x + 1 - core, group)
    z_peer = (loop, 4 * h + 2 * (1 - z) + y)
    y_peer = (loop, 4 * h + 2 * z + 1 - y)

    def h_peer(j):
        return (loop, 4 * ((h + j) % far) + 2 * z + y)

    barrier = pltpu.get_barrier_semaphore()
    peers = [x_peer, core_peer, z_peer, y_peer] + [h_peer(j) for j in range(1, far)]
    for peer in peers:
        pl.semaphore_signal(barrier, inc=1, device_id=peer, device_id_type=MESH)

    started = []

    def remote(index, src, dst, peer):
        return pltpu.make_async_remote_copy(
            src_ref=src,
            dst_ref=dst,
            send_sem=send_sem.at[index],
            recv_sem=recv_sem.at[index],
            device_id=peer,
            device_id_type=MESH,
        )

    def start(index, src, dst, peer):
        copy = remote(index, src, dst, peer)
        copy.start()
        started.append(copy)
        return copy

    own = 2 * x + z
    beside = 2 * x + 1 - z
    txt_unit, _ = unit_normalize(txt_ref[...])
    pair_own[...] = txt_unit.astype(BF16)
    pl.semaphore_wait(barrier, len(peers))
    pair_copy = start(0, pair_own, pair_in, y_peer)
    img_unit, _ = unit_normalize(img_ref[...])
    images[own] = img_unit.astype(BF16)
    z_copy = start(1, images.at[own], images.at[own], z_peer)
    x_copy = start(2, images.at[own], images.at[own], x_peer)

    device = loop * (4 * far) + group
    tally_own = tally_ref[device]
    tally_peer = tally_ref[loop * (4 * far) + 4 * h + 2 * z + 1 - y]
    has_own = jnp.minimum(tally_own, 1).astype(F32)
    has_peer = jnp.minimum(tally_peer, 1).astype(F32)

    pair_copy.wait_recv()
    texts[core, h, y] = (
        pair_own[:half].astype(F32) * has_own + pair_in[half:].astype(F32) * (1.0 - has_own)
    ).astype(BF16)
    far_copies = []
    for j in range(1, far):
        far_copies.append(start(10 + j, texts.at[core, h, y], texts.at[core, h, y], h_peer(j)))
    texts[core, h, 1 - y] = (
        pair_in[:half].astype(F32) * has_peer + pair_own[half:].astype(F32) * (1.0 - has_peer)
    ).astype(BF16)
    core_copies = [start(3, texts.at[core, h], texts.at[core, h], core_peer)]

    z_copy.wait_recv()
    x_forward = start(4, images.at[beside], images.at[beside], x_peer)

    y_forwards = []
    for j in range(1, far):
        source = (h + far - j) % far
        far_copies[j - 1].wait_recv()
        slot = texts.at[core, source, y]
        y_forwards.append(start(10 + far + j, slot, slot, y_peer))
    for j in range(1, far):
        source = (h + far - j) % far
        y_forwards[j - 1].wait_recv()
        both = texts.at[core, source]
        core_copies.append(start(10 + 2 * far + j, both, both, core_peer))
    for copy in core_copies:
        copy.wait_recv()

    sharpness = sharp_ref[0]
    shift = shift_ref[0]
    row_ids = lax.broadcasted_iota(jnp.int32, (rows, 1), 0)

    def text_block(c):
        return texts[c].reshape(far * rows, width)

    def image_step(sx, sz):
        place = 2 * sx + sz
        block = images[place]
        tally = tally_ref[(2 * sx + core) * (4 * far) + 4 * h + 2 * sz + y]
        scale = jnp.where(row_ids < tally, sharpness, 0.0)
        total = None
        for c in range(2):
            block_texts = text_block(c)
            logits = (
                lax.dot_general(
                    block, block_texts, (((1,), (1,)), ((), ())), preferred_element_type=F32
                )
                * sharpness
                + shift
            )
            pulled = 1.0 / (1.0 + jnp.exp(-logits))
            if sx is x and sz is z:
                base = h * rows
                near = base + y * half + row_ids
                later = base + (1 - y) * half + row_ids - half
                goal = jnp.where(row_ids < half, near, later)
                goal = jnp.where(core == c, goal, -1)
                columns = lax.broadcasted_iota(jnp.int32, logits.shape, 1)
                pulled = pulled - jnp.where(columns == goal, 1.0, 0.0)
            weight = (scale * pulled).astype(BF16)
            weights[c, pl.ds(pl.multiple_of(place * rows, rows), rows)] = weight
            term = jnp.dot(weight, block_texts, preferred_element_type=F32)
            total = term if total is None else total + term
        return total

    x_copy.wait_recv()
    img_send[z] = image_step(1 - x, z).astype(BF16)
    img_first = start(5, img_send.at[z], img_recv.at[z], x_peer)
    x_forward.wait_recv()
    other_z = 1 - z
    img_send[other_z] = image_step(1 - x, other_z).astype(BF16)
    img_second = start(6, img_send.at[other_z], img_recv.at[other_z], x_peer)
    img_keep[other_z] = image_step(x, other_z)
    img_keep[z] = image_step(x, z)

    all_images = images[...].reshape(4 * rows, width)

    def text_grads(c):
        return lax.dot_general(
            weights[c], all_images, (((0,), (0,)), ((), ())), preferred_element_type=F32
        )

    core_send[...] = text_grads(1 - core)
    core_copy = start(7, core_send, core_recv, core_peer)
    txt_keep[...] = text_grads(core).reshape(far, 2, half, width)

    core_copy.wait_recv()
    merged = core_recv.reshape(far, 2, half, width)
    for p in range(far):
        txt_send[p] = (txt_keep[p, 1 - y] + merged[p, 1 - y]).astype(BF16)
    y_copy = start(8, txt_send, txt_recv, y_peer)

    img_second_slot = other_z
    img_first.wait_recv()
    img_second.wait_recv()
    img_send2[...] = (img_keep[img_second_slot] + img_recv[img_second_slot].astype(F32)).astype(BF16)
    img_last = start(9, img_send2, img_recv2, z_peer)

    y_copy.wait_recv()
    back = []
    for j in range(1, far):
        goal_h = (h + j) % far
        txt_send2[j] = (
            txt_keep[goal_h, y] + merged[goal_h, y] + txt_recv[goal_h].astype(F32)
        ).astype(BF16)
        back.append(start(10 + 3 * far + j, txt_send2.at[j], txt_recv2.at[j], h_peer(j)))
    slot_sum = txt_keep[h, y] + merged[h, y] + txt_recv[h].astype(F32)

    img_last.wait_recv()
    img_sum = img_keep[z] + img_recv[z].astype(F32) + img_recv2[...].astype(F32)
    img_out[...] = project(img_ref[...], img_sum)

    for j in range(1, far):
        back[j - 1].wait_recv()
        slot_sum = slot_sum + txt_recv2[j].astype(F32)
    last_send[...] = slot_sum.astype(BF16)
    last_copy = start(10, last_send, last_recv, y_peer)
    txt_out[:half] = project(txt_ref[:half], slot_sum * has_own)
    last_copy.wait_recv()
    txt_out[half:] = project(txt_ref[half:], last_recv[...].astype(F32) * (1.0 - has_peer))

    for copy in started:
        copy.wait_send()


def per_device(far, pictures, captions, tally, sharpness, shift):
    rows, width = pictures.shape
    half = rows // 2
    vmem = pl.BlockSpec(memory_space=pltpu.VMEM)
    smem = pl.BlockSpec(memory_space=pltpu.SMEM)
    shape = jax.ShapeDtypeStruct((rows, width), BF16)
    copies = 10 + 4 * far
    return pl.pallas_call(
        functools.partial(kernel, far),
        out_shape=(shape, shape),
        in_specs=[vmem, vmem, smem, smem, smem],
        out_specs=(vmem, vmem),
        scratch_shapes=[
            pltpu.VMEM((4, rows, width), BF16),
            pltpu.VMEM((rows, width), BF16),
            pltpu.VMEM((rows, width), BF16),
            pltpu.VMEM((2, far, 2, half, width), BF16),
            pltpu.VMEM((2, 4 * rows, far * rows), BF16),
            pltpu.VMEM((2, rows, width), BF16),
            pltpu.VMEM((2, rows, width), BF16),
            pltpu.VMEM((2, rows, width), F32),
            pltpu.VMEM((rows, width), BF16),
            pltpu.VMEM((rows, width), BF16),
            pltpu.VMEM((far * rows, width), F32),
            pltpu.VMEM((far * rows, width), F32),
            pltpu.VMEM((far, 2, half, width), F32),
            pltpu.VMEM((far, half, width), BF16),
            pltpu.VMEM((far, half, width), BF16),
            pltpu.VMEM((far, half, width), BF16),
            pltpu.VMEM((far, half, width), BF16),
            pltpu.VMEM((half, width), BF16),
            pltpu.VMEM((half, width), BF16),
            pltpu.SemaphoreType.DMA((copies,)),
            pltpu.SemaphoreType.DMA((copies,)),
        ],
        compiler_params=pltpu.CompilerParams(
            collective_id=0, has_side_effects=True, vmem_limit_bytes=60 * 1024 * 1024
        ),
    )(pictures, captions, tally, sharpness, shift)


def solution(mesh):
    far = mesh.shape["group"] // 4
    spec = P(("loop", "group"), None)
    return jax.shard_map(
        functools.partial(per_device, far),
        mesh=mesh,
        in_specs=(spec, spec, P(), P(), P()),
        out_specs=(spec, spec),
        check_vma=False,
    )
```

```python
import functools

import jax
import jax.numpy as jnp
from jax import lax
from jax.experimental import pallas as pl
from jax.experimental.pallas import tpu as pltpu
from jax.sharding import PartitionSpec as P

MESH = pl.DeviceIdType.MESH
F32 = jnp.float32
BF16 = jnp.bfloat16
PIECES = 2


def unit_normalize(raw):
    values = raw.astype(F32)
    inverse = lax.rsqrt(jnp.sum(values * values, axis=1, keepdims=True) + 1e-06)
    return values * inverse, inverse


def project(raw, grads):
    unit, inverse = unit_normalize(raw)
    radial = jnp.sum(unit * grads, axis=1, keepdims=True)
    return ((grads - unit * radial) * inverse).astype(BF16)


def kernel(
    far,
    img_ref,
    txt_ref,
    tally_ref,
    sharp_ref,
    shift_ref,
    img_out,
    txt_out,
    images,
    pair_own,
    pair_in,
    texts,
    weights,
    img_keep,
    x_send,
    x_recv,
    z_send,
    z_recv,
    last_img_send,
    last_img_recv,
    core_send,
    core_recv,
    txt_keep,
    y_send,
    y_recv,
    h_send,
    h_recv,
    last_send,
    last_recv,
    send_sem,
    recv_sem,
):
    rows, width = img_ref.shape
    half = rows // 2
    piece = half // PIECES
    pieces = [slice(p * piece, (p + 1) * piece) for p in range(PIECES)]
    loop = lax.axis_index("loop")
    group = lax.axis_index("group")
    x, core = loop // 2, loop % 2
    h, z, y = group // 4, (group // 2) % 2, group % 2

    x_peer = (2 * (1 - x) + core, group)
    core_peer = (2 * x + 1 - core, group)
    z_peer = (loop, 4 * h + 2 * (1 - z) + y)
    y_peer = (loop, 4 * h + 2 * z + 1 - y)

    def h_peer(j):
        return (loop, 4 * ((h + j) % far) + 2 * z + y)

    barrier = pltpu.get_barrier_semaphore()
    peers = [x_peer, core_peer, z_peer, y_peer] + [h_peer(j) for j in range(1, far)]
    for peer in peers:
        pl.semaphore_signal(barrier, inc=1, device_id=peer, device_id_type=MESH)

    started = []

    def start(src, dst, peer):
        index = len(started)
        copy = pltpu.make_async_remote_copy(
            src_ref=src,
            dst_ref=dst,
            send_sem=send_sem.at[index],
            recv_sem=recv_sem.at[index],
            device_id=peer,
            device_id_type=MESH,
        )
        copy.start()
        started.append(copy)
        return copy

    own, beside = 2 * x + z, 2 * x + 1 - z
    across, corner = 2 * (1 - x) + z, 2 * (1 - x) + 1 - z

    txt_unit, _ = unit_normalize(txt_ref[...])
    pair_own[...] = txt_unit.astype(BF16)
    pl.semaphore_wait(barrier, len(peers))
    pair_second = []
    for p in range(PIECES):
        part = pl.ds(half + p * piece, piece)
        pair_second.append(start(pair_own.at[part], pair_in.at[part], y_peer))
    part = pl.ds(0, half)
    pair_first = start(pair_own.at[part], pair_in.at[part], y_peer)
    img_unit, _ = unit_normalize(img_ref[...])
    images[own] = img_unit.astype(BF16)
    x_copy = start(images.at[own], images.at[own], x_peer)
    z_copy = start(images.at[own], images.at[own], z_peer)

    device = loop * (4 * far) + group
    tally_own = tally_ref[device]
    tally_peer = tally_ref[loop * (4 * far) + 4 * h + 2 * z + 1 - y]
    has_own = jnp.minimum(tally_own, 1).astype(F32)
    has_peer = jnp.minimum(tally_peer, 1).astype(F32)

    far_copies = []
    for p in range(PIECES):
        pair_second[p].wait_recv()
        mine = pair_own[pieces[p]].astype(F32)
        other = pair_in[half + p * piece : half + (p + 1) * piece].astype(F32)
        texts[h, core, y, pieces[p]] = (mine * has_own + other * (1.0 - has_own)).astype(BF16)
        slot = texts.at[h, core, y, pl.ds(p * piece, piece)]
        far_copies.append([start(slot, slot, h_peer(j)) for j in range(1, far)])
    pair_first.wait_recv()
    texts[h, core, 1 - y] = (
        pair_in[:half].astype(F32) * has_peer + pair_own[half:].astype(F32) * (1.0 - has_peer)
    ).astype(BF16)
    core_copies = [start(texts.at[h, core], texts.at[h, core], core_peer)]
    y_forwards = []

    def forward_piece(p):
        copies = []
        for j in range(1, far):
            far_copies[p][j - 1].wait_recv()
            slot = texts.at[(h + far - j) % far, core, y, pl.ds(p * piece, piece)]
            copies.append(start(slot, slot, y_peer))
        y_forwards.append(copies)

    sharpness = sharp_ref[0]
    shift = shift_ref[0]
    row_ids = lax.broadcasted_iota(jnp.int32, (rows, 1), 0)

    def weigh(place, block_texts, diagonal=False):
        sx, sz = place // 2, place % 2
        tally = tally_ref[(2 * sx + core) * (4 * far) + 4 * h + 2 * sz + y]
        scale = jnp.where(row_ids < tally, sharpness, 0.0)
        logits = (
            lax.dot_general(
                images[place], block_texts, (((1,), (1,)), ((), ())), preferred_element_type=F32
            )
            * sharpness
            + shift
        )
        pulled = 1.0 / (1.0 + jnp.exp(-logits))
        if diagonal:
            goal = jnp.where(row_ids < half, y * half, (1 - y) * half - half)
            goal = goal + core * rows + row_ids
            columns = lax.broadcasted_iota(jnp.int32, logits.shape, 1)
            pulled = pulled - jnp.where(columns == goal, 1.0, 0.0)
        weight = (scale * pulled).astype(BF16)
        for c in range(2):
            weights[c, pl.ds(pl.multiple_of(place * rows, rows), rows)] = weight[
                :, c * rows : (c + 1) * rows
            ]
        return weight

    def text_grads(c):
        return lax.dot_general(
            weights[c],
            images[...].reshape(4 * rows, width),
            (((0,), (0,)), ((), ())),
            preferred_element_type=F32,
        ).reshape(2, half, width)

    def send_core(j):
        core_send[j] = text_grads(1 - core)
        copy = start(core_send.at[j], core_recv.at[j], core_peer)
        txt_keep[j] = text_grads(core)
        return copy

    def send_y(j, copy):
        copy.wait_recv()
        y_send[j] = (txt_keep[j, 1 - y] + core_recv[j, 1 - y]).astype(BF16)
        copies = []
        for p in range(PIECES):
            part = pl.ds(p * piece, piece)
            copies.append(start(y_send.at[j, part], y_recv.at[j, part], y_peer))
        txt_keep[j, y] = txt_keep[j, y] + core_recv[j, y]
        return copies

    forward_piece(0)
    x_copy.wait_recv()
    part = pl.ds(half, half)
    corner_b = start(images.at[across, part], images.at[across, part], z_peer)
    z_copy.wait_recv()
    part = pl.ds(0, half)
    corner_a = start(images.at[beside, part], images.at[beside, part], x_peer)

    core_copies[0].wait_recv()

    def near_step(place, diagonal=False):
        block_texts = texts[h].reshape(2 * rows, width)
        weight = weigh(place, block_texts, diagonal)
        img_keep[place] = jnp.dot(weight, block_texts, preferred_element_type=F32)

    near_step(own, True)
    near_step(across)
    near_step(beside)
    for p in range(1, PIECES):
        forward_piece(p)
    corner_a.wait_recv()
    corner_b.wait_recv()
    near_step(corner)
    core_sums = [send_core(0)]
    y_sums = []

    for j in range(1, far):
        for p in range(PIECES):
            y_forwards[p][j - 1].wait_recv()
        pair = texts.at[(h + far - j) % far, core]
        core_copies.append(start(pair, pair, core_peer))
    for j in range(1, far):
        y_sums.append(send_y(j - 1, core_sums[j - 1]))
        core_copies[j].wait_recv()
        block_texts = texts[(h + far - j) % far].reshape(2 * rows, width)
        for place in (corner, across, beside, own):
            weigh(place, block_texts)
        core_sums.append(send_core(j))
        if j < far - 1:
            for place in (corner, across, beside, own):
                row_range = pl.ds(pl.multiple_of(place * rows, rows), rows)
                for c in range(2):
                    img_keep[place] += jnp.dot(
                        weights[c, row_range],
                        texts[(h + far - j) % far, c].reshape(rows, width),
                        preferred_element_type=F32,
                    )

    def last_step(place):
        row_range = pl.ds(pl.multiple_of(place * rows, rows), rows)
        weight = jnp.concatenate([weights[0, row_range], weights[1, row_range]], axis=1)
        block_texts = texts[(h + 1) % far].reshape(2 * rows, width)
        return img_keep[place] + jnp.dot(weight, block_texts, preferred_element_type=F32)

    total = last_step(corner)
    x_send[1 - z] = total[:half].astype(BF16)
    z_send[1 - x] = total[half:].astype(BF16)
    x_first = [start(x_send.at[1 - z], x_recv.at[1 - z], x_peer)]
    z_first = [start(z_send.at[1 - x], z_recv.at[1 - x], z_peer)]
    total = last_step(across)
    x_send[z] = total[:half].astype(BF16)
    x_first.append(start(x_send.at[z], x_recv.at[z], x_peer))
    img_keep[across] = total
    total = last_step(beside)
    z_send[x] = total[half:].astype(BF16)
    z_first.append(start(z_send.at[x], z_recv.at[x], z_peer))
    img_keep[beside] = total

    y_sums.append(send_y(far - 1, core_sums[far - 1]))
    img_keep[own] = last_step(own)

    h_copies = [[None] * far for _ in range(PIECES)]
    for j in range(1, far):
        for p in range(PIECES):
            y_sums[j][p].wait_recv()
            part = pl.ds(p * piece, piece)
            h_send[j, pieces[p]] = (
                txt_keep[j, y, pieces[p]] + y_recv[j, pieces[p]].astype(F32)
            ).astype(BF16)
            h_copies[p][j] = start(h_send.at[j, part], h_recv.at[j, part], h_peer(far - j))

    x_first[0].wait_recv()
    last_img_send[0] = (img_keep[beside, :half] + x_recv[1 - z].astype(F32)).astype(BF16)
    last_z = start(last_img_send.at[0], last_img_recv.at[0], z_peer)
    z_first[0].wait_recv()
    last_img_send[1] = (img_keep[across, half:] + z_recv[1 - x].astype(F32)).astype(BF16)
    last_x = start(last_img_send.at[1], last_img_recv.at[1], x_peer)

    for p in range(PIECES):
        y_sums[0][p].wait_recv()
    last_copies = []
    for p in range(PIECES):
        slot_sum = txt_keep[0, y, pieces[p]] + y_recv[0, pieces[p]].astype(F32)
        for j in range(1, far):
            h_copies[p][j].wait_recv()
            slot_sum = slot_sum + h_recv[j, pieces[p]].astype(F32)
        last_send[pieces[p]] = slot_sum.astype(BF16)
        part = pl.ds(p * piece, piece)
        last_copies.append(start(last_send.at[part], last_recv.at[part], y_peer))
        txt_out[pieces[p]] = project(txt_ref[pieces[p]], slot_sum * has_own)

    x_first[1].wait_recv()
    last_z.wait_recv()
    img_sum = img_keep[own, :half] + x_recv[z].astype(F32) + last_img_recv[0].astype(F32)
    img_out[:half] = project(img_ref[:half], img_sum)
    z_first[1].wait_recv()
    last_x.wait_recv()
    img_sum = img_keep[own, half:] + z_recv[x].astype(F32) + last_img_recv[1].astype(F32)
    img_out[half:] = project(img_ref[half:], img_sum)

    for p in range(PIECES):
        last_copies[p].wait_recv()
        part = slice(half + p * piece, half + (p + 1) * piece)
        txt_out[part] = project(
            txt_ref[part], last_recv[pieces[p]].astype(F32) * (1.0 - has_peer)
        )

    for copy in started:
        copy.wait_send()


def per_device(far, pictures, captions, tally, sharpness, shift):
    rows, width = pictures.shape
    half = rows // 2
    vmem = pl.BlockSpec(memory_space=pltpu.VMEM)
    smem = pl.BlockSpec(memory_space=pltpu.SMEM)
    shape = jax.ShapeDtypeStruct((rows, width), BF16)
    copies = 16 + 4 * PIECES + far * (2 + 4 * PIECES)

    def scratch(*sizes, dtype=BF16):
        return pltpu.VMEM((*sizes, width), dtype)

    return pl.pallas_call(
        functools.partial(kernel, far),
        out_shape=(shape, shape),
        in_specs=[vmem, vmem, smem, smem, smem],
        out_specs=(vmem, vmem),
        scratch_shapes=[
            scratch(4, rows),
            scratch(rows),
            scratch(rows),
            scratch(far, 2, 2, half),
            pltpu.VMEM((2, 4 * rows, rows), BF16),
            scratch(4, rows, dtype=F32),
            scratch(2, half),
            scratch(2, half),
            scratch(2, half),
            scratch(2, half),
            scratch(2, half),
            scratch(2, half),
            scratch(far, 2, half, dtype=F32),
            scratch(far, 2, half, dtype=F32),
            scratch(far, 2, half, dtype=F32),
            scratch(far, half),
            scratch(far, half),
            scratch(far, half),
            scratch(far, half),
            scratch(half),
            scratch(half),
            pltpu.SemaphoreType.DMA((copies,)),
            pltpu.SemaphoreType.DMA((copies,)),
        ],
        compiler_params=pltpu.CompilerParams(
            collective_id=0, has_side_effects=True, vmem_limit_bytes=60 * 1024 * 1024
        ),
    )(pictures, captions, tally, sharpness, shift)


def solution(mesh):
    far = mesh.shape["group"] // 4
    spec = P(("loop", "group"), None)
    return jax.shard_map(
        functools.partial(per_device, far),
        mesh=mesh,
        in_specs=(spec, spec, P(), P(), P()),
        out_specs=(spec, spec),
        check_vma=False,
    )
```

```python
import functools

import jax
import jax.numpy as jnp
from jax import lax
from jax.experimental import pallas as pl
from jax.experimental.pallas import tpu as pltpu
from jax.sharding import PartitionSpec as P

MESH = pl.DeviceIdType.MESH
F32 = jnp.float32
BF16 = jnp.bfloat16
PIECES = 2


def unit_normalize(raw):
    values = raw.astype(F32)
    inverse = lax.rsqrt(jnp.sum(values * values, axis=1, keepdims=True) + 1e-06)
    return values * inverse, inverse


def project(raw, grads):
    unit, inverse = unit_normalize(raw)
    radial = jnp.sum(unit * grads, axis=1, keepdims=True)
    return ((grads - unit * radial) * inverse).astype(BF16)


def kernel(
    far,
    img_ref,
    txt_ref,
    tally_ref,
    sharp_ref,
    shift_ref,
    img_out,
    txt_out,
    images,
    pair_own,
    pair_in,
    texts,
    weights,
    img_keep,
    x_send,
    x_recv,
    z_send,
    z_recv,
    low_send,
    low_recv,
    high_send,
    high_recv,
    core_send,
    core_recv,
    txt_keep,
    y_send,
    y_recv,
    h_send,
    h_recv,
    last_send,
    last_recv,
    send_sem,
    recv_sem,
):
    rows, width = img_ref.shape
    half = rows // 2
    cut = rows * 3 // 4
    piece = half // PIECES
    pieces = [slice(p * piece, (p + 1) * piece) for p in range(PIECES)]
    loop = lax.axis_index("loop")
    group = lax.axis_index("group")
    x, core = loop // 2, loop % 2
    h, z, y = group // 4, (group // 2) % 2, group % 2

    x_peer = (2 * (1 - x) + core, group)
    core_peer = (2 * x + 1 - core, group)
    z_peer = (loop, 4 * h + 2 * (1 - z) + y)
    y_peer = (loop, 4 * h + 2 * z + 1 - y)

    def h_peer(j):
        return (loop, 4 * ((h + j) % far) + 2 * z + y)

    barrier = pltpu.get_barrier_semaphore()
    peers = [x_peer, core_peer, z_peer, y_peer] + [h_peer(j) for j in range(1, far)]
    for peer in peers:
        pl.semaphore_signal(barrier, inc=1, device_id=peer, device_id_type=MESH)

    started = []

    def start(src, dst, peer):
        index = len(started)
        copy = pltpu.make_async_remote_copy(
            src_ref=src,
            dst_ref=dst,
            send_sem=send_sem.at[index],
            recv_sem=recv_sem.at[index],
            device_id=peer,
            device_id_type=MESH,
        )
        copy.start()
        started.append(copy)
        return copy

    own, beside = 2 * x + z, 2 * x + 1 - z
    across, corner = 2 * (1 - x) + z, 2 * (1 - x) + 1 - z

    txt_unit, _ = unit_normalize(txt_ref[...])
    pair_own[...] = txt_unit.astype(BF16)
    pl.semaphore_wait(barrier, len(peers))
    pair_second = []
    for p in range(PIECES):
        part = pl.ds(half + p * piece, piece)
        pair_second.append(start(pair_own.at[part], pair_in.at[part], y_peer))
    part = pl.ds(0, half)
    pair_first = start(pair_own.at[part], pair_in.at[part], y_peer)
    img_unit, _ = unit_normalize(img_ref[...])
    images[own] = img_unit.astype(BF16)
    low, high = pl.ds(0, cut), pl.ds(cut, rows - cut)

    def send_image(place, part, peer):
        return start(images.at[place, part], images.at[place, part], peer)

    x_high = send_image(own, high, x_peer)
    z_low = send_image(own, low, z_peer)
    x_low = send_image(own, low, x_peer)

    device = loop * (4 * far) + group
    tally_own = tally_ref[device]
    tally_peer = tally_ref[loop * (4 * far) + 4 * h + 2 * z + 1 - y]
    has_own = jnp.minimum(tally_own, 1).astype(F32)
    has_peer = jnp.minimum(tally_peer, 1).astype(F32)

    far_copies = []
    for p in range(PIECES):
        pair_second[p].wait_recv()
        mine = pair_own[pieces[p]].astype(F32)
        other = pair_in[half + p * piece : half + (p + 1) * piece].astype(F32)
        texts[h, core, y, pieces[p]] = (mine * has_own + other * (1.0 - has_own)).astype(BF16)
        slot = texts.at[h, core, y, pl.ds(p * piece, piece)]
        far_copies.append([start(slot, slot, h_peer(j)) for j in range(1, far)])
    z_high = send_image(own, high, z_peer)
    x_high.wait_recv()
    corner_high = send_image(across, high, z_peer)
    pair_first.wait_recv()
    texts[h, core, 1 - y] = (
        pair_in[:half].astype(F32) * has_peer + pair_own[half:].astype(F32) * (1.0 - has_peer)
    ).astype(BF16)
    core_copies = [start(texts.at[h, core], texts.at[h, core], core_peer)]
    y_forwards = []

    def forward_piece(p):
        copies = []
        for j in range(1, far):
            far_copies[p][j - 1].wait_recv()
            slot = texts.at[(h + far - j) % far, core, y, pl.ds(p * piece, piece)]
            copies.append(start(slot, slot, y_peer))
        y_forwards.append(copies)

    sharpness = sharp_ref[0]
    shift = shift_ref[0]
    row_ids = lax.broadcasted_iota(jnp.int32, (rows, 1), 0)

    def weigh(place, block_texts, diagonal=False):
        sx, sz = place // 2, place % 2
        tally = tally_ref[(2 * sx + core) * (4 * far) + 4 * h + 2 * sz + y]
        scale = jnp.where(row_ids < tally, sharpness, 0.0)
        logits = (
            lax.dot_general(
                images[place], block_texts, (((1,), (1,)), ((), ())), preferred_element_type=F32
            )
            * sharpness
            + shift
        )
        pulled = 1.0 / (1.0 + jnp.exp(-logits))
        if diagonal:
            goal = jnp.where(row_ids < half, y * half, (1 - y) * half - half)
            goal = goal + core * rows + row_ids
            columns = lax.broadcasted_iota(jnp.int32, logits.shape, 1)
            pulled = pulled - jnp.where(columns == goal, 1.0, 0.0)
        weight = (scale * pulled).astype(BF16)
        for c in range(2):
            weights[c, pl.ds(pl.multiple_of(place * rows, rows), rows)] = weight[
                :, c * rows : (c + 1) * rows
            ]
        return weight

    def text_grads(c):
        return lax.dot_general(
            weights[c],
            images[...].reshape(4 * rows, width),
            (((0,), (0,)), ((), ())),
            preferred_element_type=F32,
        ).reshape(2, half, width)

    def send_core(j):
        core_send[j] = text_grads(1 - core)
        copy = start(core_send.at[j], core_recv.at[j], core_peer)
        txt_keep[j] = text_grads(core)
        return copy

    def send_y(j, copy):
        copy.wait_recv()
        y_send[j] = (txt_keep[j, 1 - y] + core_recv[j, 1 - y]).astype(BF16)
        copies = []
        for p in range(PIECES):
            part = pl.ds(p * piece, piece)
            copies.append(start(y_send.at[j, part], y_recv.at[j, part], y_peer))
        txt_keep[j, y] = txt_keep[j, y] + core_recv[j, y]
        return copies

    z_low.wait_recv()
    corner_low = send_image(beside, low, x_peer)

    core_copies[0].wait_recv()

    def near_step(place, diagonal=False):
        block_texts = texts[h].reshape(2 * rows, width)
        weight = weigh(place, block_texts, diagonal)
        img_keep[place] = jnp.dot(weight, block_texts, preferred_element_type=F32)

    near_step(own, True)
    forward_piece(0)
    x_low.wait_recv()
    near_step(across)
    for p in range(1, PIECES):
        forward_piece(p)
    z_high.wait_recv()
    near_step(beside)
    corner_low.wait_recv()
    corner_high.wait_recv()
    near_step(corner)
    core_sums = [send_core(0)]
    y_sums = []

    for j in range(1, far):
        for p in range(PIECES):
            y_forwards[p][j - 1].wait_recv()
        pair = texts.at[(h + far - j) % far, core]
        core_copies.append(start(pair, pair, core_peer))
    for j in range(1, far - 1):
        y_sums.append(send_y(j - 1, core_sums[j - 1]))
        core_copies[j].wait_recv()
        block_texts = texts[(h + far - j) % far].reshape(2 * rows, width)
        for place in (corner, across, beside, own):
            weight = weigh(place, block_texts)
            img_keep[place] += jnp.dot(weight, block_texts, preferred_element_type=F32)
        core_sums.append(send_core(j))

    y_sums.append(send_y(far - 2, core_sums[far - 2]))
    core_copies[far - 1].wait_recv()

    def last_texts():
        return texts[(h + 1) % far].reshape(2 * rows, width)

    def last_step(place, weight):
        return img_keep[place] + jnp.dot(weight, last_texts(), preferred_element_type=F32)

    def stored(place):
        row_range = pl.ds(pl.multiple_of(place * rows, rows), rows)
        return jnp.concatenate([weights[0, row_range], weights[1, row_range]], axis=1)

    total = last_step(corner, weigh(corner, last_texts()))
    x_send[1 - z] = total[:cut].astype(BF16)
    x_first = [start(x_send.at[1 - z], x_recv.at[1 - z], x_peer)]
    z_send[1 - x] = total[cut:].astype(BF16)
    z_first = [start(z_send.at[1 - x], z_recv.at[1 - x], z_peer)]
    for place in (across, beside, own):
        weigh(place, last_texts())
    core_sums.append(send_core(far - 1))
    total = last_step(across, stored(across))
    x_send[z] = total[:cut].astype(BF16)
    x_first.append(start(x_send.at[z], x_recv.at[z], x_peer))
    img_keep[across] = total
    total = last_step(beside, stored(beside))
    z_send[x] = total[cut:].astype(BF16)
    z_first.append(start(z_send.at[x], z_recv.at[x], z_peer))
    img_keep[beside] = total

    y_sums.append(send_y(far - 1, core_sums[far - 1]))
    img_keep[own] = last_step(own, stored(own))

    h_copies = [[None] * far for _ in range(PIECES)]
    for j in range(1, far):
        for p in range(PIECES):
            y_sums[j][p].wait_recv()
            part = pl.ds(p * piece, piece)
            h_send[j, pieces[p]] = (
                txt_keep[j, y, pieces[p]] + y_recv[j, pieces[p]].astype(F32)
            ).astype(BF16)
            h_copies[p][j] = start(h_send.at[j, part], h_recv.at[j, part], h_peer(far - j))

    z_first[0].wait_recv()
    high_send[...] = (img_keep[across, cut:] + z_recv[1 - x].astype(F32)).astype(BF16)
    last_x = start(high_send, high_recv, x_peer)
    x_first[0].wait_recv()
    low_send[...] = (img_keep[beside, :cut] + x_recv[1 - z].astype(F32)).astype(BF16)
    last_z = start(low_send, low_recv, z_peer)

    for p in range(PIECES):
        y_sums[0][p].wait_recv()
    last_copies = []
    for p in range(PIECES):
        slot_sum = txt_keep[0, y, pieces[p]] + y_recv[0, pieces[p]].astype(F32)
        for j in range(1, far):
            h_copies[p][j].wait_recv()
            slot_sum = slot_sum + h_recv[j, pieces[p]].astype(F32)
        last_send[pieces[p]] = slot_sum.astype(BF16)
        part = pl.ds(p * piece, piece)
        last_copies.append(start(last_send.at[part], last_recv.at[part], y_peer))
        txt_out[pieces[p]] = project(txt_ref[pieces[p]], slot_sum * has_own)

    z_first[1].wait_recv()
    last_x.wait_recv()
    img_sum = img_keep[own, cut:] + z_recv[x].astype(F32) + high_recv[...].astype(F32)
    img_out[cut:] = project(img_ref[cut:], img_sum)
    x_first[1].wait_recv()
    last_z.wait_recv()
    img_sum = img_keep[own, :cut] + x_recv[z].astype(F32) + low_recv[...].astype(F32)
    img_out[:cut] = project(img_ref[:cut], img_sum)

    for p in range(PIECES):
        last_copies[p].wait_recv()
        part = slice(half + p * piece, half + (p + 1) * piece)
        txt_out[part] = project(
            txt_ref[part], last_recv[pieces[p]].astype(F32) * (1.0 - has_peer)
        )

    for copy in started:
        copy.wait_send()


def per_device(far, pictures, captions, tally, sharpness, shift):
    rows, width = pictures.shape
    half = rows // 2
    cut = rows * 3 // 4
    vmem = pl.BlockSpec(memory_space=pltpu.VMEM)
    smem = pl.BlockSpec(memory_space=pltpu.SMEM)
    shape = jax.ShapeDtypeStruct((rows, width), BF16)
    copies = 16 + 4 * PIECES + far * (2 + 4 * PIECES)

    def scratch(*sizes, dtype=BF16):
        return pltpu.VMEM((*sizes, width), dtype)

    return pl.pallas_call(
        functools.partial(kernel, far),
        out_shape=(shape, shape),
        in_specs=[vmem, vmem, smem, smem, smem],
        out_specs=(vmem, vmem),
        scratch_shapes=[
            scratch(4, rows),
            scratch(rows),
            scratch(rows),
            scratch(far, 2, 2, half),
            pltpu.VMEM((2, 4 * rows, rows), BF16),
            scratch(4, rows, dtype=F32),
            scratch(2, cut),
            scratch(2, cut),
            scratch(2, rows - cut),
            scratch(2, rows - cut),
            scratch(cut),
            scratch(cut),
            scratch(rows - cut),
            scratch(rows - cut),
            scratch(far, 2, half, dtype=F32),
            scratch(far, 2, half, dtype=F32),
            scratch(far, 2, half, dtype=F32),
            scratch(far, half),
            scratch(far, half),
            scratch(far, half),
            scratch(far, half),
            scratch(half),
            scratch(half),
            pltpu.SemaphoreType.DMA((copies,)),
            pltpu.SemaphoreType.DMA((copies,)),
        ],
        compiler_params=pltpu.CompilerParams(
            collective_id=0, has_side_effects=True, vmem_limit_bytes=60 * 1024 * 1024
        ),
    )(pictures, captions, tally, sharpness, shift)


def solution(mesh):
    far = mesh.shape["group"] // 4
    spec = P(("loop", "group"), None)
    return jax.shard_map(
        functools.partial(per_device, far),
        mesh=mesh,
        in_specs=(spec, spec, P(), P(), P()),
        out_specs=(spec, spec),
        check_vma=False,
    )
```

```python
import functools

import jax
import jax.numpy as jnp
from jax import lax
from jax.experimental import pallas as pl
from jax.experimental.pallas import tpu as pltpu
from jax.sharding import PartitionSpec as P

MESH = pl.DeviceIdType.MESH
F32 = jnp.float32
BF16 = jnp.bfloat16
PIECES = 4


def unit_normalize(raw):
    values = raw.astype(F32)
    inverse = lax.rsqrt(jnp.sum(values * values, axis=1, keepdims=True) + 1e-06)
    return values * inverse, inverse


def project(raw, grads):
    unit, inverse = unit_normalize(raw)
    radial = jnp.sum(unit * grads, axis=1, keepdims=True)
    return ((grads - unit * radial) * inverse).astype(BF16)


def kernel(
    far,
    img_ref,
    txt_ref,
    tally_ref,
    sharp_ref,
    shift_ref,
    img_out,
    txt_out,
    images,
    pair_own,
    pair_in,
    texts,
    weights,
    img_keep,
    x_send,
    x_recv,
    z_send,
    z_recv,
    low_send,
    low_recv,
    high_send,
    high_recv,
    core_send,
    core_recv,
    txt_keep,
    y_send,
    y_recv,
    h_send,
    h_recv,
    last_send,
    last_recv,
    send_sem,
    recv_sem,
):
    rows, width = img_ref.shape
    half = rows // 2
    cut = rows * 5 // 8
    piece = half // PIECES
    pieces = [slice(p * piece, (p + 1) * piece) for p in range(PIECES)]
    loop = lax.axis_index("loop")
    group = lax.axis_index("group")
    x, core = loop // 2, loop % 2
    h, z, y = group // 4, (group // 2) % 2, group % 2

    x_peer = (2 * (1 - x) + core, group)
    core_peer = (2 * x + 1 - core, group)
    z_peer = (loop, 4 * h + 2 * (1 - z) + y)
    y_peer = (loop, 4 * h + 2 * z + 1 - y)

    def h_peer(j):
        return (loop, 4 * ((h + j) % far) + 2 * z + y)

    barrier = pltpu.get_barrier_semaphore()
    peers = [x_peer, core_peer, z_peer, y_peer] + [h_peer(j) for j in range(1, far)]
    for peer in peers:
        pl.semaphore_signal(barrier, inc=1, device_id=peer, device_id_type=MESH)

    started = []

    def start(src, dst, peer):
        index = len(started)
        copy = pltpu.make_async_remote_copy(
            src_ref=src,
            dst_ref=dst,
            send_sem=send_sem.at[index],
            recv_sem=recv_sem.at[index],
            device_id=peer,
            device_id_type=MESH,
        )
        copy.start()
        started.append(copy)
        return copy

    own, beside = 2 * x + z, 2 * x + 1 - z
    across, corner = 2 * (1 - x) + z, 2 * (1 - x) + 1 - z

    txt_unit, _ = unit_normalize(txt_ref[...])
    pair_own[...] = txt_unit.astype(BF16)
    pl.semaphore_wait(barrier, len(peers))
    pair_second = []
    for p in range(PIECES):
        part = pl.ds(half + p * piece, piece)
        pair_second.append(start(pair_own.at[part], pair_in.at[part], y_peer))
    part = pl.ds(0, half)
    pair_first = start(pair_own.at[part], pair_in.at[part], y_peer)
    img_unit, _ = unit_normalize(img_ref[...])
    images[own] = img_unit.astype(BF16)
    low, high = pl.ds(0, cut), pl.ds(cut, rows - cut)

    def send_image(place, part, peer):
        return start(images.at[place, part], images.at[place, part], peer)

    x_high = send_image(own, high, x_peer)
    z_low = send_image(own, low, z_peer)
    x_low = send_image(own, low, x_peer)

    device = loop * (4 * far) + group
    tally_own = tally_ref[device]
    tally_peer = tally_ref[loop * (4 * far) + 4 * h + 2 * z + 1 - y]
    has_own = jnp.minimum(tally_own, 1).astype(F32)
    has_peer = jnp.minimum(tally_peer, 1).astype(F32)

    far_copies = []
    for p in range(PIECES):
        pair_second[p].wait_recv()
        mine = pair_own[pieces[p]].astype(F32)
        other = pair_in[half + p * piece : half + (p + 1) * piece].astype(F32)
        texts[h, core, y, pieces[p]] = (mine * has_own + other * (1.0 - has_own)).astype(BF16)
        slot = texts.at[h, core, y, pl.ds(p * piece, piece)]
        far_copies.append([start(slot, slot, h_peer(j)) for j in range(1, far)])
    z_high = send_image(own, high, z_peer)
    x_high.wait_recv()
    corner_high = send_image(across, high, z_peer)
    pair_first.wait_recv()
    texts[h, core, 1 - y] = (
        pair_in[:half].astype(F32) * has_peer + pair_own[half:].astype(F32) * (1.0 - has_peer)
    ).astype(BF16)
    core_copies = [start(texts.at[h, core], texts.at[h, core], core_peer)]
    y_forwards = []

    def forward_piece(p):
        copies = []
        for j in range(1, far):
            far_copies[p][j - 1].wait_recv()
            slot = texts.at[(h + far - j) % far, core, y, pl.ds(p * piece, piece)]
            copies.append(start(slot, slot, y_peer))
        y_forwards.append(copies)

    sharpness = sharp_ref[0]
    shift = shift_ref[0]
    row_ids = lax.broadcasted_iota(jnp.int32, (rows, 1), 0)

    def weigh(place, block_texts, diagonal=False):
        sx, sz = place // 2, place % 2
        tally = tally_ref[(2 * sx + core) * (4 * far) + 4 * h + 2 * sz + y]
        scale = jnp.where(row_ids < tally, sharpness, 0.0)
        logits = (
            lax.dot_general(
                images[place], block_texts, (((1,), (1,)), ((), ())), preferred_element_type=F32
            )
            * sharpness
            + shift
        )
        pulled = 1.0 / (1.0 + jnp.exp(-logits))
        if diagonal:
            goal = jnp.where(row_ids < half, y * half, (1 - y) * half - half)
            goal = goal + core * rows + row_ids
            columns = lax.broadcasted_iota(jnp.int32, logits.shape, 1)
            pulled = pulled - jnp.where(columns == goal, 1.0, 0.0)
        weight = (scale * pulled).astype(BF16)
        for c in range(2):
            weights[c, pl.ds(pl.multiple_of(place * rows, rows), rows)] = weight[
                :, c * rows : (c + 1) * rows
            ]
        return weight

    def text_grads(c):
        return lax.dot_general(
            weights[c],
            images[...].reshape(4 * rows, width),
            (((0,), (0,)), ((), ())),
            preferred_element_type=F32,
        ).reshape(2, half, width)

    def send_core(j):
        core_send[j] = text_grads(1 - core)
        copy = start(core_send.at[j], core_recv.at[j], core_peer)
        txt_keep[j] = text_grads(core)
        return copy

    def send_y(j, copy):
        copy.wait_recv()
        y_send[j] = (txt_keep[j, 1 - y] + core_recv[j, 1 - y]).astype(BF16)
        copies = []
        for p in range(PIECES):
            part = pl.ds(p * piece, piece)
            copies.append(start(y_send.at[j, part], y_recv.at[j, part], y_peer))
        txt_keep[j, y] = txt_keep[j, y] + core_recv[j, y]
        return copies

    z_low.wait_recv()
    corner_low = send_image(beside, low, x_peer)

    core_copies[0].wait_recv()

    def near_step(place, diagonal=False):
        block_texts = texts[h].reshape(2 * rows, width)
        weight = weigh(place, block_texts, diagonal)
        img_keep[place] = jnp.dot(weight, block_texts, preferred_element_type=F32)

    near_step(own, True)
    forward_piece(0)
    x_low.wait_recv()
    near_step(across)
    for p in range(1, PIECES):
        forward_piece(p)
    z_high.wait_recv()
    near_step(beside)
    corner_low.wait_recv()
    corner_high.wait_recv()
    near_step(corner)
    core_sums = [send_core(0)]
    y_sums = []

    for j in range(1, far):
        for p in range(PIECES):
            y_forwards[p][j - 1].wait_recv()
        pair = texts.at[(h + far - j) % far, core]
        core_copies.append(start(pair, pair, core_peer))
    for j in range(1, far - 1):
        y_sums.append(send_y(j - 1, core_sums[j - 1]))
        core_copies[j].wait_recv()
        block_texts = texts[(h + far - j) % far].reshape(2 * rows, width)
        for place in (corner, across, beside, own):
            weight = weigh(place, block_texts)
            img_keep[place] += jnp.dot(weight, block_texts, preferred_element_type=F32)
        core_sums.append(send_core(j))

    y_sums.append(send_y(far - 2, core_sums[far - 2]))
    core_copies[far - 1].wait_recv()

    def last_texts():
        return texts[(h + 1) % far].reshape(2 * rows, width)

    def last_step(place, weight):
        return img_keep[place] + jnp.dot(weight, last_texts(), preferred_element_type=F32)

    def stored(place):
        row_range = pl.ds(pl.multiple_of(place * rows, rows), rows)
        return jnp.concatenate([weights[0, row_range], weights[1, row_range]], axis=1)

    total = last_step(corner, weigh(corner, last_texts()))
    x_send[1 - z] = total[:cut].astype(BF16)
    x_first = [start(x_send.at[1 - z], x_recv.at[1 - z], x_peer)]
    z_send[1 - x] = total[cut:].astype(BF16)
    z_first = [start(z_send.at[1 - x], z_recv.at[1 - x], z_peer)]
    for place in (across, beside, own):
        weigh(place, last_texts())
    core_sums.append(send_core(far - 1))
    total = last_step(across, stored(across))
    x_send[z] = total[:cut].astype(BF16)
    x_first.append(start(x_send.at[z], x_recv.at[z], x_peer))
    img_keep[across] = total
    total = last_step(beside, stored(beside))
    z_send[x] = total[cut:].astype(BF16)
    z_first.append(start(z_send.at[x], z_recv.at[x], z_peer))
    img_keep[beside] = total

    y_sums.append(send_y(far - 1, core_sums[far - 1]))
    img_keep[own] = last_step(own, stored(own))

    h_copies = [[None] * far for _ in range(PIECES)]
    for j in range(1, far):
        for p in range(PIECES):
            y_sums[j][p].wait_recv()
            part = pl.ds(p * piece, piece)
            h_send[j, pieces[p]] = (
                txt_keep[j, y, pieces[p]] + y_recv[j, pieces[p]].astype(F32)
            ).astype(BF16)
            h_copies[p][j] = start(h_send.at[j, part], h_recv.at[j, part], h_peer(far - j))

    z_first[0].wait_recv()
    high_send[...] = (img_keep[across, cut:] + z_recv[1 - x].astype(F32)).astype(BF16)
    last_x = start(high_send, high_recv, x_peer)
    x_first[0].wait_recv()
    low_send[...] = (img_keep[beside, :cut] + x_recv[1 - z].astype(F32)).astype(BF16)
    last_z = start(low_send, low_recv, z_peer)

    for p in range(PIECES):
        y_sums[0][p].wait_recv()
    last_copies = []
    for p in range(PIECES):
        slot_sum = txt_keep[0, y, pieces[p]] + y_recv[0, pieces[p]].astype(F32)
        for j in range(1, far):
            h_copies[p][j].wait_recv()
            slot_sum = slot_sum + h_recv[j, pieces[p]].astype(F32)
        last_send[pieces[p]] = slot_sum.astype(BF16)
        part = pl.ds(p * piece, piece)
        last_copies.append(start(last_send.at[part], last_recv.at[part], y_peer))
        txt_out[pieces[p]] = project(txt_ref[pieces[p]], slot_sum * has_own)

    z_first[1].wait_recv()
    last_x.wait_recv()
    img_sum = img_keep[own, cut:] + z_recv[x].astype(F32) + high_recv[...].astype(F32)
    img_out[cut:] = project(img_ref[cut:], img_sum)
    x_first[1].wait_recv()
    last_z.wait_recv()
    img_sum = img_keep[own, :cut] + x_recv[z].astype(F32) + low_recv[...].astype(F32)
    img_out[:cut] = project(img_ref[:cut], img_sum)

    for p in range(PIECES):
        last_copies[p].wait_recv()
        part = slice(half + p * piece, half + (p + 1) * piece)
        txt_out[part] = project(
            txt_ref[part], last_recv[pieces[p]].astype(F32) * (1.0 - has_peer)
        )

    for copy in started:
        copy.wait_send()


def per_device(far, pictures, captions, tally, sharpness, shift):
    rows, width = pictures.shape
    half = rows // 2
    cut = rows * 5 // 8
    vmem = pl.BlockSpec(memory_space=pltpu.VMEM)
    smem = pl.BlockSpec(memory_space=pltpu.SMEM)
    shape = jax.ShapeDtypeStruct((rows, width), BF16)
    copies = 16 + 4 * PIECES + far * (2 + 4 * PIECES)

    def scratch(*sizes, dtype=BF16):
        return pltpu.VMEM((*sizes, width), dtype)

    return pl.pallas_call(
        functools.partial(kernel, far),
        out_shape=(shape, shape),
        in_specs=[vmem, vmem, smem, smem, smem],
        out_specs=(vmem, vmem),
        scratch_shapes=[
            scratch(4, rows),
            scratch(rows),
            scratch(rows),
            scratch(far, 2, 2, half),
            pltpu.VMEM((2, 4 * rows, rows), BF16),
            scratch(4, rows, dtype=F32),
            scratch(2, cut),
            scratch(2, cut),
            scratch(2, rows - cut),
            scratch(2, rows - cut),
            scratch(cut),
            scratch(cut),
            scratch(rows - cut),
            scratch(rows - cut),
            scratch(far, 2, half, dtype=F32),
            scratch(far, 2, half, dtype=F32),
            scratch(far, 2, half, dtype=F32),
            scratch(far, half),
            scratch(far, half),
            scratch(far, half),
            scratch(far, half),
            scratch(half),
            scratch(half),
            pltpu.SemaphoreType.DMA((copies,)),
            pltpu.SemaphoreType.DMA((copies,)),
        ],
        compiler_params=pltpu.CompilerParams(
            collective_id=0, has_side_effects=True, vmem_limit_bytes=(16 + 8 * far) << 20
        ),
    )(pictures, captions, tally, sharpness, shift)


def solution(mesh):
    far = mesh.shape["group"] // 4
    spec = P(("loop", "group"), None)
    return jax.shard_map(
        functools.partial(per_device, far),
        mesh=mesh,
        in_specs=(spec, spec, P(), P(), P()),
        out_specs=(spec, spec),
        check_vma=False,
    )
```

```python
import functools

import jax
import jax.numpy as jnp
from jax import lax
from jax.experimental import pallas as pl
from jax.experimental.pallas import tpu as pltpu
from jax.sharding import PartitionSpec as P

MESH = pl.DeviceIdType.MESH
F32 = jnp.float32
BF16 = jnp.bfloat16
PIECES = 4


def unit_normalize(raw):
    values = raw.astype(F32)
    inverse = lax.rsqrt(jnp.sum(values * values, axis=1, keepdims=True) + 1e-06)
    return values * inverse, inverse


def project(raw, grads):
    unit, inverse = unit_normalize(raw)
    radial = jnp.sum(unit * grads, axis=1, keepdims=True)
    return ((grads - unit * radial) * inverse).astype(BF16)


def kernel(
    far,
    img_ref,
    txt_ref,
    tally_ref,
    sharp_ref,
    shift_ref,
    img_out,
    txt_out,
    images,
    pair_own,
    pair_in,
    texts,
    weights,
    img_keep,
    x_send,
    x_recv,
    z_send,
    z_recv,
    low_send,
    low_recv,
    high_send,
    high_recv,
    core_send,
    core_recv,
    txt_keep,
    y_send,
    y_recv,
    h_send,
    h_recv,
    last_send,
    last_recv,
    send_sem,
    recv_sem,
):
    rows, width = img_ref.shape
    half = rows // 2
    cut = rows * 5 // 8
    piece = half // PIECES
    pieces = [slice(p * piece, (p + 1) * piece) for p in range(PIECES)]
    loop = lax.axis_index("loop")
    group = lax.axis_index("group")
    x, core = loop // 2, loop % 2
    h, z, y = group // 4, (group // 2) % 2, group % 2

    x_peer = (2 * (1 - x) + core, group)
    core_peer = (2 * x + 1 - core, group)
    z_peer = (loop, 4 * h + 2 * (1 - z) + y)
    y_peer = (loop, 4 * h + 2 * z + 1 - y)

    def h_peer(j):
        return (loop, 4 * ((h + j) % far) + 2 * z + y)

    barrier = pltpu.get_barrier_semaphore()
    peers = [x_peer, core_peer, z_peer, y_peer] + [h_peer(j) for j in range(1, far)]
    for peer in peers:
        pl.semaphore_signal(barrier, inc=1, device_id=peer, device_id_type=MESH)

    started = []

    def start(src, dst, peer):
        index = len(started)
        copy = pltpu.make_async_remote_copy(
            src_ref=src,
            dst_ref=dst,
            send_sem=send_sem.at[index],
            recv_sem=recv_sem.at[index],
            device_id=peer,
            device_id_type=MESH,
        )
        copy.start()
        started.append(copy)
        return copy

    own, beside = 2 * x + z, 2 * x + 1 - z
    across, corner = 2 * (1 - x) + z, 2 * (1 - x) + 1 - z

    txt_unit, _ = unit_normalize(txt_ref[...])
    pair_own[...] = txt_unit.astype(BF16)
    pl.semaphore_wait(barrier, len(peers))
    pair_second = []
    for p in range(PIECES):
        part = pl.ds(half + p * piece, piece)
        pair_second.append(start(pair_own.at[part], pair_in.at[part], y_peer))
    part = pl.ds(0, half)
    pair_first = start(pair_own.at[part], pair_in.at[part], y_peer)
    img_unit, _ = unit_normalize(img_ref[...])
    images[own] = img_unit.astype(BF16)
    low, high = pl.ds(0, cut), pl.ds(cut, rows - cut)

    def send_image(place, part, peer):
        return start(images.at[place, part], images.at[place, part], peer)

    x_high = send_image(own, high, x_peer)
    z_low = send_image(own, low, z_peer)
    x_low = send_image(own, low, x_peer)

    device = loop * (4 * far) + group
    tally_own = tally_ref[device]
    tally_peer = tally_ref[loop * (4 * far) + 4 * h + 2 * z + 1 - y]
    has_own = jnp.minimum(tally_own, 1).astype(F32)
    has_peer = jnp.minimum(tally_peer, 1).astype(F32)

    far_copies = []
    for p in range(PIECES):
        pair_second[p].wait_recv()
        mine = pair_own[pieces[p]].astype(F32)
        other = pair_in[half + p * piece : half + (p + 1) * piece].astype(F32)
        texts[h, core, y, pieces[p]] = (mine * has_own + other * (1.0 - has_own)).astype(BF16)
        slot = texts.at[h, core, y, pl.ds(p * piece, piece)]
        far_copies.append([start(slot, slot, h_peer(j)) for j in range(1, far)])
    z_high = send_image(own, high, z_peer)
    x_high.wait_recv()
    corner_high = send_image(across, high, z_peer)
    pair_first.wait_recv()
    texts[h, core, 1 - y] = (
        pair_in[:half].astype(F32) * has_peer + pair_own[half:].astype(F32) * (1.0 - has_peer)
    ).astype(BF16)
    core_copies = [start(texts.at[h, core], texts.at[h, core], core_peer)]
    y_forwards = []

    def forward_piece(p):
        copies = []
        for j in range(1, far):
            far_copies[p][j - 1].wait_recv()
            slot = texts.at[(h + far - j) % far, core, y, pl.ds(p * piece, piece)]
            copies.append(start(slot, slot, y_peer))
        y_forwards.append(copies)

    sharpness = sharp_ref[0]
    shift = shift_ref[0]
    row_ids = lax.broadcasted_iota(jnp.int32, (rows, 1), 0)

    def weigh(place, block_texts, diagonal=False):
        sx, sz = place // 2, place % 2
        tally = tally_ref[(2 * sx + core) * (4 * far) + 4 * h + 2 * sz + y]
        scale = jnp.where(row_ids < tally, sharpness, 0.0)
        logits = (
            lax.dot_general(
                images[place], block_texts, (((1,), (1,)), ((), ())), preferred_element_type=F32
            )
            * sharpness
            + shift
        )
        pulled = 1.0 / (1.0 + jnp.exp(-logits))
        if diagonal:
            goal = jnp.where(row_ids < half, y * half, (1 - y) * half - half)
            goal = goal + core * rows + row_ids
            columns = lax.broadcasted_iota(jnp.int32, logits.shape, 1)
            pulled = pulled - jnp.where(columns == goal, 1.0, 0.0)
        weight = (scale * pulled).astype(BF16)
        for c in range(2):
            weights[c, pl.ds(pl.multiple_of(place * rows, rows), rows)] = weight[
                :, c * rows : (c + 1) * rows
            ]
        return weight

    def text_grads(c):
        return lax.dot_general(
            weights[c],
            images[...].reshape(4 * rows, width),
            (((0,), (0,)), ((), ())),
            preferred_element_type=F32,
        ).reshape(2, half, width)

    def send_core(j):
        core_send[j] = text_grads(1 - core)
        copy = start(core_send.at[j], core_recv.at[j], core_peer)
        txt_keep[j] = text_grads(core)
        return copy

    def send_y(j, copy):
        copy.wait_recv()
        y_send[j] = (txt_keep[j, 1 - y] + core_recv[j, 1 - y]).astype(BF16)
        copies = []
        for p in range(PIECES):
            part = pl.ds(p * piece, piece)
            copies.append(start(y_send.at[j, part], y_recv.at[j, part], y_peer))
        txt_keep[j, y] = txt_keep[j, y] + core_recv[j, y]
        return copies

    z_low.wait_recv()
    corner_low = send_image(beside, low, x_peer)

    core_copies[0].wait_recv()

    def near_step(place, diagonal=False):
        block_texts = texts[h].reshape(2 * rows, width)
        weight = weigh(place, block_texts, diagonal)
        img_keep[place] = jnp.dot(weight, block_texts, preferred_element_type=F32)

    near_step(own, True)
    forward_piece(0)
    x_low.wait_recv()
    near_step(across)
    for p in range(1, PIECES):
        forward_piece(p)
    z_high.wait_recv()
    near_step(beside)
    corner_low.wait_recv()
    corner_high.wait_recv()
    near_step(corner)
    core_sums = [send_core(0)]
    y_sums = []

    for j in range(1, far):
        for p in range(PIECES):
            y_forwards[p][j - 1].wait_recv()
        pair = texts.at[(h + far - j) % far, core]
        core_copies.append(start(pair, pair, core_peer))
    for j in range(1, far - 1):
        y_sums.append(send_y(j - 1, core_sums[j - 1]))
        core_copies[j].wait_recv()
        block_texts = texts[(h + far - j) % far].reshape(2 * rows, width)
        for place in (corner, across, beside, own):
            weight = weigh(place, block_texts)
            img_keep[place] += jnp.dot(weight, block_texts, preferred_element_type=F32)
        core_sums.append(send_core(j))

    y_sums.append(send_y(far - 2, core_sums[far - 2]))
    core_copies[far - 1].wait_recv()

    def last_texts():
        return texts[(h + 1) % far].reshape(2 * rows, width)

    def last_step(place, weight):
        return img_keep[place] + jnp.dot(weight, last_texts(), preferred_element_type=F32)

    def stored(place):
        row_range = pl.ds(pl.multiple_of(place * rows, rows), rows)
        return jnp.concatenate([weights[0, row_range], weights[1, row_range]], axis=1)

    for place in (corner, across, beside, own):
        weigh(place, last_texts())
    core_sums.append(send_core(far - 1))
    total = last_step(corner, stored(corner))
    x_send[1 - z] = total[:cut].astype(BF16)
    x_first = [start(x_send.at[1 - z], x_recv.at[1 - z], x_peer)]
    z_send[1 - x] = total[cut:].astype(BF16)
    z_first = [start(z_send.at[1 - x], z_recv.at[1 - x], z_peer)]
    total = last_step(across, stored(across))
    x_send[z] = total[:cut].astype(BF16)
    x_first.append(start(x_send.at[z], x_recv.at[z], x_peer))
    img_keep[across] = total
    total = last_step(beside, stored(beside))
    z_send[x] = total[cut:].astype(BF16)
    z_first.append(start(z_send.at[x], z_recv.at[x], z_peer))
    img_keep[beside] = total

    y_sums.append(send_y(far - 1, core_sums[far - 1]))
    img_keep[own] = last_step(own, stored(own))

    h_copies = [[None] * far for _ in range(PIECES)]
    for j in range(1, far):
        for p in range(PIECES):
            y_sums[j][p].wait_recv()
            part = pl.ds(p * piece, piece)
            h_send[j, pieces[p]] = (
                txt_keep[j, y, pieces[p]] + y_recv[j, pieces[p]].astype(F32)
            ).astype(BF16)
            h_copies[p][j] = start(h_send.at[j, part], h_recv.at[j, part], h_peer(far - j))

    z_first[0].wait_recv()
    high_send[...] = (img_keep[across, cut:] + z_recv[1 - x].astype(F32)).astype(BF16)
    last_x = start(high_send, high_recv, x_peer)
    x_first[0].wait_recv()
    low_send[...] = (img_keep[beside, :cut] + x_recv[1 - z].astype(F32)).astype(BF16)
    last_z = start(low_send, low_recv, z_peer)

    for p in range(PIECES):
        y_sums[0][p].wait_recv()
    last_copies = []
    for p in range(PIECES):
        slot_sum = txt_keep[0, y, pieces[p]] + y_recv[0, pieces[p]].astype(F32)
        for j in range(1, far):
            h_copies[p][j].wait_recv()
            slot_sum = slot_sum + h_recv[j, pieces[p]].astype(F32)
        last_send[pieces[p]] = slot_sum.astype(BF16)
        part = pl.ds(p * piece, piece)
        last_copies.append(start(last_send.at[part], last_recv.at[part], y_peer))
        txt_out[pieces[p]] = project(txt_ref[pieces[p]], slot_sum * has_own)

    z_first[1].wait_recv()
    last_x.wait_recv()
    img_sum = img_keep[own, cut:] + z_recv[x].astype(F32) + high_recv[...].astype(F32)
    img_out[cut:] = project(img_ref[cut:], img_sum)
    x_first[1].wait_recv()
    last_z.wait_recv()
    img_sum = img_keep[own, :cut] + x_recv[z].astype(F32) + low_recv[...].astype(F32)
    img_out[:cut] = project(img_ref[:cut], img_sum)

    for p in range(PIECES):
        last_copies[p].wait_recv()
        part = slice(half + p * piece, half + (p + 1) * piece)
        txt_out[part] = project(
            txt_ref[part], last_recv[pieces[p]].astype(F32) * (1.0 - has_peer)
        )

    for copy in started:
        copy.wait_send()


def per_device(far, pictures, captions, tally, sharpness, shift):
    rows, width = pictures.shape
    half = rows // 2
    cut = rows * 5 // 8
    vmem = pl.BlockSpec(memory_space=pltpu.VMEM)
    smem = pl.BlockSpec(memory_space=pltpu.SMEM)
    shape = jax.ShapeDtypeStruct((rows, width), BF16)
    copies = 16 + 4 * PIECES + far * (2 + 4 * PIECES)

    def scratch(*sizes, dtype=BF16):
        return pltpu.VMEM((*sizes, width), dtype)

    return pl.pallas_call(
        functools.partial(kernel, far),
        out_shape=(shape, shape),
        in_specs=[vmem, vmem, smem, smem, smem],
        out_specs=(vmem, vmem),
        scratch_shapes=[
            scratch(4, rows),
            scratch(rows),
            scratch(rows),
            scratch(far, 2, 2, half),
            pltpu.VMEM((2, 4 * rows, rows), BF16),
            scratch(4, rows, dtype=F32),
            scratch(2, cut),
            scratch(2, cut),
            scratch(2, rows - cut),
            scratch(2, rows - cut),
            scratch(cut),
            scratch(cut),
            scratch(rows - cut),
            scratch(rows - cut),
            scratch(far, 2, half, dtype=F32),
            scratch(far, 2, half, dtype=F32),
            scratch(far, 2, half, dtype=F32),
            scratch(far, half),
            scratch(far, half),
            scratch(far, half),
            scratch(far, half),
            scratch(half),
            scratch(half),
            pltpu.SemaphoreType.DMA((copies,)),
            pltpu.SemaphoreType.DMA((copies,)),
        ],
        compiler_params=pltpu.CompilerParams(
            collective_id=0, has_side_effects=True, vmem_limit_bytes=(16 + 8 * far) << 20
        ),
    )(pictures, captions, tally, sharpness, shift)


def solution(mesh):
    far = mesh.shape["group"] // 4
    spec = P(("loop", "group"), None)
    return jax.shard_map(
        functools.partial(per_device, far),
        mesh=mesh,
        in_specs=(spec, spec, P(), P(), P()),
        out_specs=(spec, spec),
        check_vma=False,
    )
```
